128 devices in a mesh: ch: 16 (over x, y), sx: 4 (over z), sy: 2 (over core).
Axes of the slice: x: 4, y: 4, z: 4, core: 2. Of those that a mesh axis runs over, the one named last changes fastest.
Arguments:
- volume: bfloat16 [512, 2, 16, 256], P('ch', None, 'sx', 'sy'), may hold values from -6 to 6
- kernel: bfloat16 [27, 512, 512], P(None, 'ch'), may hold values from -0.0546875 to 0.0546875
- cotangent: bfloat16 [512, 2, 16, 256], P('ch', None, 'sx', 'sy'), may hold values from -6 to 6
Outputs:
- response: bfloat16 [512, 2, 16, 256], P('ch', None, 'sx', 'sy')
- volume_grad: bfloat16 [512, 2, 16, 256], P('ch', None, 'sx', 'sy')
- kernel_grad: float32 [27, 512, 512], P(None, 'ch')
The draws below stay inside these ranges and needn't reach their ends.
All inputs are finite; a program needn't handle non-finite values.
Results may differ from the reference program's by a relative error of at most 0.001.
Values may be sent and summed in bfloat16 or wider, within the bound.
A program may use at most 128 MiB of HBM per device.

```python
import jax
import jax.numpy as jnp

CIN = 512
COUT = 512
DEPTH = 2
NX = 16
NY = 256


def shard_levels(rng, extent, shards, low, largest):
    gain = 1.0
    for axis_at, blocks in shards:
        steps = jax.random.uniform(jax.random.fold_in(jax.random.fold_in(rng, 6), axis_at), (blocks,), jnp.float32, low / len(shards), largest / len(shards))
        gain = gain * jnp.repeat(jnp.exp(steps), extent[axis_at] // blocks).reshape((-1,) + (1,) * (len(extent) - 1 - axis_at))
    return gain


def scatter_about(own_key, shape, scale, most, cuts=(), kind=jnp.bfloat16):
    loudness = shard_levels(own_key, shape, cuts, -0.22, 0.18) if cuts else 1.0
    values = jax.random.normal(own_key, shape, jnp.float32) * scale * loudness
    return jnp.minimum(jnp.maximum(values, -most), most).astype(kind)


def setup_inputs(seed: int = 0) -> dict:
    arg_keys = jax.random.split(jax.random.key(seed), 4)
    return {
        "volume": scatter_about(arg_keys[0], (CIN, DEPTH, NX, NY), 1.0, 6.0, ((0, 16), (2, 4), (3, 2))),
        "kernel": scatter_about(arg_keys[1], (27, CIN, COUT), (27 * CIN) ** -0.5, 0.0546875, ((1, 16),)),
        "cotangent": scatter_about(arg_keys[2], (COUT, DEPTH, NX, NY), 1.0, 6.0, ((0, 16), (2, 4), (3, 2))),
    }


def pad_cells(field):
    return jnp.pad(field, ((0, 0), (1, 1), (1, 1), (1, 1)))

def reference(volume, kernel, cotangent):
    depth = volume.shape[1]
    wide = volume.shape[2]
    tall = volume.shape[3]
    padded_in = pad_cells(volume).astype(jnp.float32)
    padded_grad = pad_cells(cotangent).astype(jnp.float32)
    grad_full = cotangent.astype(jnp.float32)
    weights = kernel.astype(jnp.float32)
    forward_sum = jnp.zeros((kernel.shape[2], depth, wide, tall), jnp.float32)
    backward_sum = jnp.zeros((kernel.shape[1], depth, wide, tall), jnp.float32)
    grads = []
    for step_z in range(3):
        for step_x in range(3):
            for step_y in range(3):
                tap = step_z * 9 + step_x * 3 + step_y
                window = padded_in[:, step_z:step_z + depth, step_x:step_x + wide, step_y:step_y + tall]
                forward_sum = forward_sum + jnp.einsum('io,izxy->ozxy', weights[tap], window)
                back_window = padded_grad[:, 2 - step_z:2 - step_z + depth, 2 - step_x:2 - step_x + wide, 2 - step_y:2 - step_y + tall]
                backward_sum = backward_sum + jnp.einsum('io,ozxy->izxy', weights[tap], back_window)
                grads.append(jnp.einsum('izxy,ozxy->io', window, grad_full))
    scale = 1.0 / jnp.sqrt(jnp.float32(depth * wide * tall))
    kernel_grad = jnp.stack(grads, axis=0) * scale
    return (forward_sum.astype(jnp.bfloat16), backward_sum.astype(jnp.bfloat16), kernel_grad)
```

```python
import functools

import jax
import jax.numpy as jnp
from jax import lax
from jax.experimental import pallas as pl
from jax.experimental.pallas import tpu as pltpu
from jax.sharding import PartitionSpec as P

MESH = pl.DeviceIdType.MESH
F32 = jnp.float32
BF16 = jnp.bfloat16


def nearby(i):
    return i + 1 - 2 * (i % 2), 3 - i, (i + 2) % 4


def body(
    scale, v_ref, c_ref, k_ref, resp_ref, vgrad_ref, kgrad_ref,
    rows32, full, other, edges, left, right, taps, kpart, kcore, kone, ktwo, kpiece,
    part, one, two, send_sem, recv_sem,
):
    c = lax.axis_index("ch")
    z = lax.axis_index("sx")
    p = lax.axis_index("sy")
    x, y = c // 4, c % 4
    x1, x3, x2 = nearby(x)
    y1, y3, y2 = nearby(y)
    z1, z3, z2 = nearby(z)
    up, down = (z + 1) % 4, (z + 3) % 4
    q = 1 - p

    def at(tx=None, ty=None, tz=None, tp=None):
        tx = x if tx is None else tx
        ty = y if ty is None else ty
        return {"ch": tx * 4 + ty, "sx": z if tz is None else tz, "sy": p if tp is None else tp}

    partners = [
        at(tx=x1), at(tx=x3), at(tx=x2), at(ty=y1), at(ty=y3), at(tz=z1), at(tz=z3),
        at(tp=q), at(tz=z1, tp=q), at(tz=z3, tp=q),
    ]
    barrier = pltpu.get_barrier_semaphore()
    for who in partners:
        pl.semaphore_signal(barrier, inc=1, device_id=who, device_id_type=MESH)

    for a, ref, g in ((0, v_ref, x), (1, c_ref, y)):
        rows32[a] = ref[...].astype(F32)
        for d in range(2):
            for b in range(4):
                block = rows32[a, pl.ds(d * 4 + b, 32, stride=8), :]
                full[a, d, g, :, 128 * (b + 1) : 128 * (b + 2)] = block.astype(BF16)
    pl.semaphore_wait(barrier, len(partners))

    count = [0]
    sends = []

    def push(src, dst, who):
        n = count[0]
        count[0] += 1
        copy = pltpu.make_async_remote_copy(
            src_ref=src, dst_ref=dst, send_sem=send_sem.at[n], recv_sem=recv_sem.at[n],
            device_id=who, device_id_type=MESH,
        )
        copy.start()
        sends.append(copy)
        return copy

    halo = []
    for a, g in ((0, x), (1, y)):
        low = full.at[a, :, g, :, pl.ds(128, 128)]
        high = full.at[a, :, g, :, pl.ds(512, 128)]
        halo.append(push(high, full.at[a, :, g, :, pl.ds(0, 128)], at(tz=up)))
        halo.append(push(low, full.at[a, :, g, :, pl.ds(640, 128)], at(tz=down)))
        halo.append(push(high, edges.at[a, 0], at(tz=up, tp=q)))
        halo.append(push(low, edges.at[a, 1], at(tz=down, tp=q)))
        halo.append(push(full.at[a, :, g, :, pl.ds(128, 512)], other.at[a], at(tp=q)))

    half = pl.ds(16 * p, 16)
    last = jnp.minimum(7 * z + 6, 26)
    tap_in = []
    for g in (x1, x3, x2):
        lanes = pl.ds(pl.multiple_of(128 * g, 128), 128)
        tap_in.append(push(k_ref.at[pl.ds(7 * z, 6), half, lanes], taps.at[pl.ds(7 * z, 6), x, half], at(tx=g)))
        tap_in.append(push(k_ref.at[last, half, lanes], taps.at[7 * z + 6, x, half], at(tx=g)))
    lanes = pl.ds(pl.multiple_of(128 * x, 128), 128)
    own = [
        pltpu.make_async_copy(k_ref.at[pl.ds(7 * z, 6), half, lanes], taps.at[pl.ds(7 * z, 6), x, half], send_sem.at[100]),
        pltpu.make_async_copy(k_ref.at[last, half, lanes], taps.at[7 * z + 6, x, half], send_sem.at[101]),
    ]
    for copy in own:
        copy.start()

    lane = lax.broadcasted_iota(jnp.int32, (64, 128), 1)
    has_low, has_high = z > 0, z < 3
    for a, g in ((0, x), (1, y)):
        for copy in halo[5 * a : 5 * a + 5]:
            copy.wait_recv()
        for b, ok in ((0, has_low), (5, has_high)):
            block = full[a, :, g, :, 128 * b : 128 * b + 128]
            full[a, :, g, :, 128 * b : 128 * b + 128] = jnp.where(ok, block, jnp.zeros_like(block))
        packed = jnp.zeros((64, 128), F32)
        for b in range(6):
            if b == 0:
                block = jnp.where(has_low, edges[a, 0].reshape(64, 128).astype(F32), 0.0)
            elif b == 5:
                block = jnp.where(has_high, edges[a, 1].reshape(64, 128).astype(F32), 0.0)
            else:
                block = other[a, :, :, 128 * b - 128 : 128 * b].reshape(64, 128).astype(F32)
            here = block if b == 0 else pltpu.roll(block, b, 1)
            there = pltpu.roll(block, b + 1, 1)
            packed = jnp.where(lane == b, jnp.where(p == 0, here, there), packed)
        full[a, :, g, :, 768:896] = packed.astype(BF16).reshape(2, 32, 128)

    def gather(ref, mine, one_way, other_way, to_one, to_other, cut):
        first = push(ref(mine, None), ref(mine, None), to_one)
        second = push(ref(mine, None), ref(mine, None), to_other)
        return first, second

    def whole(a, g):
        return full.at[a, :, g]

    def front(a, g):
        return full.at[a, :, g, :, pl.ds(0, 512)]

    def back(a, g):
        return full.at[a, :, g, :, pl.ds(512, 384)]

    rings = ((0, x, x1, x3, at(tx=x1), at(tx=x3)), (1, y, y1, y3, at(ty=y1), at(ty=y3)))
    near = []
    for a, g, g1, g3, to1, to3 in rings:
        near.append((push(whole(a, g), whole(a, g), to1), push(whole(a, g), whole(a, g), to3)))
    far = []
    for a, g, g1, g3, to1, to3 in rings:
        near[a][0].wait_recv()
        f = push(front(a, g1), front(a, g1), to3)
        near[a][1].wait_recv()
        far.append((f, push(back(a, g3), back(a, g3), to1)))

    for copy in own:
        copy.wait()
    for copy in tap_in:
        copy.wait_recv()

    def tap_piece(t, g0, n):
        return taps.at[pl.ds(7 * t, 7), pl.ds(g0, n), half]

    t1 = push(tap_piece(z, 0, 4), tap_piece(z, 0, 4), at(tz=z1))
    t3 = push(tap_piece(z, 0, 4), tap_piece(z, 0, 4), at(tz=z3))

    lane = lax.broadcasted_iota(jnp.int32, (256, 128), 1)
    for a in range(2):
        for copy in far[a]:
            copy.wait_recv()
        packed = full[a, :, :, :, 768:896].reshape(256, 128).astype(F32)
        for b in range(6):
            block = full[a, :, :, :, 128 * b : 128 * b + 128].reshape(256, 128).astype(F32)
            col = packed if b == 0 else pltpu.roll(packed, 128 - b, 1)
            shifted = jnp.where(lane == 0, jnp.where(p == 1, col, 0.0), pltpu.roll(block, 1, 1))
            left[a, :, 128 * b : 128 * b + 128] = shifted.astype(BF16)
            col = pltpu.roll(packed, 127 - b, 1)
            shifted = jnp.where(lane == 127, jnp.where(p == 0, col, 0.0), pltpu.roll(block, 127, 1))
            right[a, :, 128 * b : 128 * b + 128] = shifted.astype(BF16)

    t1.wait_recv()
    t1f = push(tap_piece(z1, 0, 2), tap_piece(z1, 0, 2), at(tz=z3))
    t3.wait_recv()
    t3f = push(tap_piece(z3, 2, 2), tap_piece(z3, 2, 2), at(tz=z1))

    def window(a, dy, dx):
        if dy == 1:
            return full[a, :, :, :, 128 * dx : 128 * dx + 512].reshape(256, 512)
        return (left if dy == 0 else right)[a, :, 128 * dx : 128 * dx + 512]

    cot = full[1, :, :, :, 128:640].reshape(256, 512)
    for dx in range(3):
        for dy in range(3):
            r = lax.dot_general(window(0, dy, dx), cot, (((1,), (1,)), ((), ())), preferred_element_type=F32)
            t = dx * 3 + dy
            kpart[t] = r[:128, 128:].reshape(4, 32, 128)
            kpart[9 + t] = (r[:128, :128] + r[128:, 128:]).reshape(4, 32, 128)
            kpart[18 + t] = r[128:, :128].reshape(4, 32, 128)
    kpart[27] = jnp.zeros((4, 32, 128), F32)
    their_half = pl.ds(pl.multiple_of(16 * q, 16), 16)
    core_sum = push(kpart.at[:, :, their_half], kcore, at(tp=q))

    t1f.wait_recv()
    t3f.wait_recv()
    tap_core = push(taps.at[:, :, half], taps.at[:, :, half], at(tp=q))

    my_half = pl.ds(pl.multiple_of(16 * p, 16), 16)
    core_sum.wait_recv()
    kcore[...] += kpart[:, :, my_half, :]

    def k_first(h, me, to, q1):
        rows = pl.ds(8 * h, 8)
        a0 = push(kcore.at[pl.ds(7 * q1, 7), :, rows], kone.at[h, 0], to)
        a1 = push(kcore.at[pl.ds(7 * z2, 7), :, rows], kone.at[h, 1], to)
        return a0, a1

    ka = k_first(0, z, at(tz=z3), z3)
    kb = k_first(1, z, at(tz=z1), z1)

    tap_core.wait_recv()

    def filt(dx, dy):
        t = dx * 3 + dy
        w0 = taps[t].reshape(128, 128)
        w1 = taps[9 + t].reshape(128, 128)
        w2 = taps[18 + t].reshape(128, 128)
        return jnp.concatenate([jnp.concatenate([w1, w0], 1), jnp.concatenate([w2, w1], 1)], 0)

    acc = jnp.zeros((256, 512), F32)
    for dx in range(3):
        for dy in range(3):
            acc += jnp.dot(filt(dx, dy), window(1, 2 - dy, 2 - dx), preferred_element_type=F32)
    part[1] = acc.reshape(2, 4, 32, 512)

    def first(a, h, to, g1, g2):
        cells = pl.ds(256 * h, 256)
        a0 = push(part.at[a, :, g1, :, cells], one.at[a, h, 0], to)
        a1 = push(part.at[a, :, g2, :, cells], one.at[a, h, 1], to)
        return a0, a1

    ba = first(1, 0, at(tx=x3), x3, x2)
    bb = first(1, 1, at(tx=x1), x1, x2)

    for copy in ka + kb:
        copy.wait_recv()
    kone[0, 1] += kcore[pl.ds(7 * z1, 7), :, 0:8, :]
    ka2 = push(kone.at[0, 1], ktwo.at[0], at(tz=z1))
    kone[1, 1] += kcore[pl.ds(7 * z3, 7), :, 8:16, :]
    kb2 = push(kone.at[1, 1], ktwo.at[1], at(tz=z3))

    acc = jnp.zeros((256, 512), F32)
    for dx in range(3):
        for dy in range(3):
            acc += lax.dot_general(
                filt(dx, dy), window(0, dy, dx), (((0,), (0,)), ((), ())), preferred_element_type=F32
            )
    part[0] = acc.reshape(2, 4, 32, 512)
    aa = first(0, 0, at(ty=y3), y3, y2)
    ab = first(0, 1, at(ty=y1), y1, y2)

    ka2.wait_recv()
    kb2.wait_recv()
    for h in range(2):
        kpiece[:, :, 8 * h : 8 * h + 8, :] = (
            kcore[pl.ds(7 * z, 7), :, 8 * h : 8 * h + 8, :] + kone[h, 0] + ktwo[h]
        ) * scale
    my_lanes = pl.ds(pl.multiple_of(128 * x, 128), 128)
    my_taps = pl.ds(7 * z, 7)
    there = kgrad_ref.at[my_taps, my_half, my_lanes]
    kx = [push(kpiece.at[:, g], there, at(tx=g)) for g in (x1, x3, x2)]
    kgrad_ref[my_taps, my_half, my_lanes] = kpiece[:, pl.ds(x, 1), :, :].reshape(7, 16, 128)

    def second(a, h, to, g, copies):
        for copy in copies:
            copy.wait_recv()
        one[a, h, 1] += part[a, :, g, :, 256 * h : 256 * h + 256]
        return push(one.at[a, h, 1], two.at[a, h], to)

    ba2 = second(1, 0, at(tx=x1), x1, ba)
    bb2 = second(1, 1, at(tx=x3), x3, bb)
    aa2 = second(0, 0, at(ty=y1), y1, aa)
    ab2 = second(0, 1, at(ty=y3), y3, ab)

    for copy in kx:
        copy.wait_recv()

    def k_piece(t, r, n):
        return kgrad_ref.at[pl.ds(7 * t, 7), pl.ds(pl.multiple_of(16 * p + r, 8), n), :]

    g1 = push(k_piece(z, 0, 16), k_piece(z, 0, 16), at(tz=z1))
    g3 = push(k_piece(z, 0, 16), k_piece(z, 0, 16), at(tz=z3))
    gc = [push(k_piece(z, 0, 16), k_piece(z, 0, 16), at(tp=q))]

    def finish(a, g, out_ref, copies):
        for h, copy in enumerate(copies):
            copy.wait_recv()
            for d in range(2):
                total = part[a, d, pl.ds(g, 1), :, 256 * h : 256 * h + 256].reshape(32, 256) + one[a, h, 0, d] + two[a, h, d]
                for b in range(2):
                    rows32[a, pl.ds(d * 4 + 2 * h + b, 32, stride=8), :] = total[:, 128 * b : 128 * b + 128]
        out_ref[...] = rows32[a].astype(BF16)

    finish(1, x, vgrad_ref, (ba2, bb2))
    finish(0, y, resp_ref, (aa2, ab2))

    g1.wait_recv()
    g1f = push(k_piece(z1, 0, 8), k_piece(z1, 0, 8), at(tz=z3))
    gc.append(push(k_piece(z1, 0, 16), k_piece(z1, 0, 16), at(tp=q)))
    g3.wait_recv()
    g3f = push(k_piece(z3, 8, 8), k_piece(z3, 8, 8), at(tz=z1))
    gc.append(push(k_piece(z3, 0, 16), k_piece(z3, 0, 16), at(tp=q)))
    g1f.wait_recv()
    g3f.wait_recv()
    gc.append(push(k_piece(z2, 0, 16), k_piece(z2, 0, 16), at(tp=q)))
    for copy in gc:
        copy.wait_recv()
    for copy in sends:
        copy.wait_send()


def shards(volume, kernel, cotangent):
    cells = 2 * 16 * 256
    scale = 1.0 / float(cells) ** 0.5
    vmem = pl.BlockSpec(memory_space=pltpu.VMEM)
    resp, vgrad, kgrad = pl.pallas_call(
        functools.partial(body, scale),
        out_shape=(
            jax.ShapeDtypeStruct((256, 128), BF16),
            jax.ShapeDtypeStruct((256, 128), BF16),
            jax.ShapeDtypeStruct((28, 32, 512), F32),
        ),
        in_specs=[vmem, vmem, pl.BlockSpec(memory_space=pl.ANY)],
        out_specs=(vmem, vmem, vmem),
        scratch_shapes=[
            pltpu.VMEM((2, 256, 128), F32),
            pltpu.VMEM((2, 2, 4, 32, 896), BF16),
            pltpu.VMEM((2, 2, 32, 512), BF16),
            pltpu.VMEM((2, 2, 2, 32, 128), BF16),
            pltpu.VMEM((2, 256, 768), BF16),
            pltpu.VMEM((2, 256, 768), BF16),
            pltpu.VMEM((28, 4, 32, 128), BF16),
            pltpu.VMEM((28, 4, 32, 128), F32),
            pltpu.VMEM((28, 4, 16, 128), F32),
            pltpu.VMEM((2, 2, 7, 4, 8, 128), F32),
            pltpu.VMEM((2, 7, 4, 8, 128), F32),
            pltpu.VMEM((7, 4, 16, 128), F32),
            pltpu.VMEM((2, 2, 4, 32, 512), F32),
            pltpu.VMEM((2, 2, 2, 2, 32, 256), F32),
            pltpu.VMEM((2, 2, 2, 32, 256), F32),
            pltpu.SemaphoreType.DMA((102,)),
            pltpu.SemaphoreType.DMA((102,)),
        ],
        compiler_params=pltpu.CompilerParams(
            collective_id=0, has_side_effects=True, vmem_limit_bytes=48 * 1024 * 1024
        ),
    )(volume.reshape(256, 128), cotangent.reshape(256, 128), kernel)
    return (resp.reshape(volume.shape), vgrad.reshape(volume.shape), kgrad[:27])


def solution(mesh):
    in_specs = (P("ch", None, "sx", "sy"), P(None, "ch", None), P("ch", None, "sx", "sy"))
    out_specs = (P("ch", None, "sx", "sy"), P("ch", None, "sx", "sy"), P(None, "ch", None))
    return jax.shard_map(shards, mesh=mesh, in_specs=in_specs, out_specs=out_specs, check_vma=False)
```

```python
import functools

import jax
import jax.numpy as jnp
from jax import lax
from jax.experimental import pallas as pl
from jax.experimental.pallas import tpu as pltpu
from jax.sharding import PartitionSpec as P

MESH = pl.DeviceIdType.MESH
F32 = jnp.float32
BF16 = jnp.bfloat16
SPAN = 86.0
ORDER = [(dz, dx, dy) for dy in (1, 0, 2) for dz in range(3) for dx in range(3)]


def nearby(i):
    return i + 1 - 2 * (i % 2), 3 - i, (i + 2) % 4


def encode(values):
    top = jnp.max(jnp.abs(values), axis=0)
    unit = (jnp.maximum(top, 1e-30) * 1.01).astype(BF16)
    gain = SPAN / unit.astype(F32)
    return jnp.exp(values * gain[None]).astype(BF16), unit


def decode(code, unit):
    return jnp.log(code.astype(F32)) * (unit.astype(F32) * (1.0 / SPAN))[None]


def body(
    scale, v_ref, c_ref, k_ref, resp_ref, vgrad_ref, kcode_ref,
    bricks, rows32, full, other, left, right, taps, kpart, kcore, rsend, rland, fin,
    part, one, two, send_sem, recv_sem, load_sem,
):
    c = lax.axis_index("ch")
    z = lax.axis_index("sx")
    p = lax.axis_index("sy")
    x, y = c // 4, c % 4
    x1, x3, x2 = nearby(x)
    y1, y3, y2 = nearby(y)
    z1, z3, z2 = nearby(z)
    up, down = (z + 1) % 4, (z + 3) % 4
    q = 1 - p

    def at(tx=None, ty=None, tz=None, tp=None):
        tx = x if tx is None else tx
        ty = y if ty is None else ty
        return {"ch": tx * 4 + ty, "sx": z if tz is None else tz, "sy": p if tp is None else tp}

    partners = [at(tx=a, tz=b) for a in (x2, x1, x3, x) for b in (z2, z1, z3, z)][:-1]
    partners += [at(ty=y2), at(ty=y1), at(ty=y3), at(tp=q)]
    barrier = pltpu.get_barrier_semaphore()
    for who in partners:
        pl.semaphore_signal(barrier, inc=1, device_id=who, device_id_type=MESH)

    half = pl.ds(pl.multiple_of(16 * p, 16), 16)
    their_half = pl.ds(pl.multiple_of(16 * q, 16), 16)
    last = jnp.minimum(7 * z + 6, 26)
    lanes = pl.ds(pl.multiple_of(128 * x, 128), 128)
    loads = [
        pltpu.make_async_copy(v_ref, bricks.at[0], load_sem.at[0]),
        pltpu.make_async_copy(c_ref, bricks.at[1], load_sem.at[1]),
        pltpu.make_async_copy(k_ref.at[pl.ds(7 * z, 6), half, lanes], taps.at[pl.ds(7 * z, 6), x, half], load_sem.at[2]),
        pltpu.make_async_copy(k_ref.at[last, half, lanes], taps.at[7 * z + 6, x, half], load_sem.at[3]),
    ]
    for copy in loads:
        copy.start()

    for a, g in ((0, x), (1, y)):
        loads[a].wait()
        rows32[a] = bricks[a].astype(F32)
        for d in range(2):
            for b in range(4):
                block = rows32[a, pl.ds(d * 4 + b, 32, stride=8), :]
                full[a, d, g, :, 128 * (b + 1) : 128 * (b + 2)] = block.astype(BF16)
    pl.semaphore_wait(barrier, len(partners))

    count = [0]
    sends = []

    def push(src, dst, who):
        n = count[0]
        count[0] += 1
        copy = pltpu.make_async_remote_copy(
            src_ref=src, dst_ref=dst, send_sem=send_sem.at[n], recv_sem=recv_sem.at[n],
            device_id=who, device_id_type=MESH,
        )
        copy.start()
        sends.append(copy)
        return copy

    def sent(copy):
        copy.wait_send()
        sends[:] = [s for s in sends if s is not copy]

    def cells(a, g, first, n):
        return full.at[a, :, g, :, pl.ds(128 * first, 128 * n)]

    vol_in = {}
    for k, g in (("2", x2), ("1", x1), ("3", x3), ("0", x)):
        vol_in[k] = [
            push(cells(0, x, 4, 1), cells(0, x, 0, 1), at(tx=g, tz=up)),
            push(cells(0, x, 1, 1), cells(0, x, 5, 1), at(tx=g, tz=down)),
        ]
        if k != "0":
            vol_in[k].append(push(cells(0, x, 1, 4), cells(0, x, 1, 4), at(tx=g)))
    cot_in = [push(cells(1, y, 1, 4), cells(1, y, 1, 4), at(ty=g)) for g in (y2, y1, y3)]

    tap_in = []
    for g in (x2, x1, x3):
        away = pl.ds(pl.multiple_of(128 * g, 128), 128)
        tap_in.append(push(k_ref.at[pl.ds(7 * z, 6), half, away], taps.at[pl.ds(7 * z, 6), x, half], at(tx=g)))
        tap_in.append(push(k_ref.at[last, half, away], taps.at[7 * z + 6, x, half], at(tx=g)))

    cross_v = []
    for k, g in (("0", x), ("1", x1), ("3", x3), ("2", x2)):
        for copy in vol_in[k]:
            copy.wait_recv()
        cross_v.append(push(full.at[0, :, g], other.at[0, :, g], at(tp=q)))
    for copy in cot_in:
        copy.wait_recv()
    every = pl.ds(0, 4)
    cot_edges = [
        push(full.at[1, :, every, :, pl.ds(512, 128)], full.at[1, :, every, :, pl.ds(0, 128)], at(tz=up)),
        push(full.at[1, :, every, :, pl.ds(128, 128)], full.at[1, :, every, :, pl.ds(640, 128)], at(tz=down)),
    ]

    def clear(ref, a):
        @pl.when(z == 0)
        def _():
            ref[a, :, :, :, 0:128] = jnp.zeros((2, 4, 32, 128), BF16)

        @pl.when(z == 3)
        def _():
            ref[a, :, :, :, 640:768] = jnp.zeros((2, 4, 32, 128), BF16)

    for copy in cross_v:
        sent(copy)
    clear(full, 0)

    def window(a, dy, dx):
        if dy == 1:
            return full[a, :, :, :, 128 * dx : 128 * dx + 512].reshape(256, 512)
        return (left if dy == 0 else right)[a, :, 128 * dx : 128 * dx + 512]

    lane = lax.broadcasted_iota(jnp.int32, (256, 128), 1)

    def shift(a):
        for b in range(6):
            mine = full[a, :, :, :, 128 * b : 128 * b + 128].reshape(256, 128).astype(F32)
            theirs = other[a, :, :, :, 128 * b : 128 * b + 128].reshape(256, 128).astype(F32)
            before = jnp.where(lane == 127, jnp.where(p == 1, theirs, 0.0), mine)
            after = jnp.where(lane == 0, jnp.where(p == 0, theirs, 0.0), mine)
            left[a, :, 128 * b : 128 * b + 128] = pltpu.roll(before, 1, 1).astype(BF16)
            right[a, :, 128 * b : 128 * b + 128] = pltpu.roll(after, 127, 1).astype(BF16)

    cot = full[1, :, :, :, 128:640].reshape(256, 512)
    core_in = []
    kpart[27] = jnp.zeros((4, 32, 128), F32)
    for s, dy in enumerate((1, 0, 2)):
        if s == 1:
            for copy in cross_v:
                copy.wait_recv()
            clear(other, 0)
            shift(0)
        for dx in range(3):
            r = lax.dot_general(window(0, dy, dx), cot, (((1,), (1,)), ((), ())), preferred_element_type=F32)
            kpart[9 * s + dx] = r[:128, 128:].reshape(4, 32, 128)
            kpart[9 * s + 3 + dx] = (r[:128, :128] + r[128:, 128:]).reshape(4, 32, 128)
            kpart[9 * s + 6 + dx] = r[128:, :128].reshape(4, 32, 128)
        span = pl.ds(9 * s, 9 if s < 2 else 10)
        core_in.append(push(kpart.at[span, :, their_half], kcore.at[span], at(tp=q)))

    for copy in loads[2:]:
        copy.wait()
    for copy in tap_in:
        copy.wait_recv()

    def tap_piece(t, g0, n):
        return taps.at[pl.ds(7 * t, 7), pl.ds(g0, n), half]

    t1 = push(tap_piece(z, 0, 4), tap_piece(z, 0, 4), at(tz=z1))
    t3 = push(tap_piece(z, 0, 4), tap_piece(z, 0, 4), at(tz=z3))

    for copy in core_in:
        copy.wait_recv()
    z_in = []
    for n, g in enumerate((z2, z1, z3)):
        span = pl.ds(7 * g, 7)
        total = (kcore[span] + kpart[span, :, half, :]).reshape(28, 16, 128)
        code, unit = encode(total)
        rsend[n, 0:28] = code
        rsend[n, 28] = unit
        z_in.append(push(rsend.at[n], rland.at[n], at(tz=g)))

    for copy in cot_edges:
        copy.wait_recv()
    cross_c = push(full.at[1], other.at[1], at(tp=q))
    t1.wait_recv()
    t1f = push(tap_piece(z1, 0, 2), tap_piece(z1, 0, 2), at(tz=z3))
    t3.wait_recv()
    t3f = push(tap_piece(z3, 2, 2), tap_piece(z3, 2, 2), at(tz=z1))
    cross_c.wait_recv()
    for copy in [cross_c] + cot_edges:
        sent(copy)
    clear(full, 1)
    clear(other, 1)
    shift(1)
    t1f.wait_recv()
    t3f.wait_recv()
    tap_core = push(taps.at[:, :, half], taps.at[:, :, half], at(tp=q))
    tap_core.wait_recv()

    def filt(dx, dy):
        t = dx * 3 + dy
        w0 = taps[t].reshape(128, 128)
        w1 = taps[9 + t].reshape(128, 128)
        w2 = taps[18 + t].reshape(128, 128)
        return jnp.concatenate([jnp.concatenate([w1, w0], 1), jnp.concatenate([w2, w1], 1)], 0)

    def first(a, h, to, g1, g2):
        cut = pl.ds(256 * h, 256)
        a0 = push(part.at[a, :, g1, :, cut], one.at[a, h, 0], to)
        a1 = push(part.at[a, :, g2, :, cut], one.at[a, h, 1], to)
        return a0, a1

    acc = jnp.zeros((256, 512), F32)
    for dx in range(3):
        for dy in range(3):
            acc += jnp.dot(filt(dx, dy), window(1, 2 - dy, 2 - dx), preferred_element_type=F32)
    part[1] = acc.reshape(2, 4, 32, 512)
    ba = first(1, 0, at(tx=x3), x3, x2)
    bb = first(1, 1, at(tx=x1), x1, x2)

    for copy in z_in:
        copy.wait_recv()
    mine = pl.ds(7 * z, 7)
    total = (kcore[mine] + kpart[mine, :, half, :]).reshape(28, 16, 128)
    for n in range(3):
        total = total + decode(rland[n, 0:28], rland[n, 28])
    total = (total * scale).reshape(7, 4, 16, 128)
    for g in range(4):
        code, unit = encode(total[:, g])
        fin[g, 0:7] = code
        fin[g, 7] = unit
    spread = {}
    for kz, gz in (("2", z2), ("1", z1), ("3", z3), ("0", z)):
        for kx, gx in (("2", x2), ("1", x1), ("3", x3), ("0", x)):
            if kz + kx != "00":
                there = kcode_ref.at[z, x, :, half, :]
                spread[kz + kx] = push(fin.at[gx], there, at(tx=gx, tz=gz))
    stores = [pltpu.make_async_copy(fin.at[x], kcode_ref.at[z, x, :, half, :], load_sem.at[4])]
    stores[0].start()

    acc = jnp.zeros((256, 512), F32)
    for dx in range(3):
        for dy in range(3):
            acc += lax.dot_general(
                filt(dx, dy), window(0, dy, dx), (((0,), (0,)), ((), ())), preferred_element_type=F32
            )
    part[0] = acc.reshape(2, 4, 32, 512)
    aa = first(0, 0, at(ty=y3), y3, y2)
    ab = first(0, 1, at(ty=y1), y1, y2)

    def second(a, h, to, g, copies):
        for copy in copies:
            copy.wait_recv()
        one[a, h, 1] += part[a, :, g, :, 256 * h : 256 * h + 256]
        return push(one.at[a, h, 1], two.at[a, h], to)

    def finish(a, g, out_ref, copies):
        for h, copy in enumerate(copies):
            copy.wait_recv()
            for d in range(2):
                total = part[a, d, pl.ds(g, 1), :, 256 * h : 256 * h + 256].reshape(32, 256) + one[a, h, 0, d] + two[a, h, d]
                for b in range(2):
                    rows32[a, pl.ds(d * 4 + 2 * h + b, 32, stride=8), :] = total[:, 128 * b : 128 * b + 128]
        bricks[a] = rows32[a].astype(BF16)
        stores.append(pltpu.make_async_copy(bricks.at[a], out_ref, load_sem.at[5 + a]))
        stores[-1].start()

    ba2 = second(1, 0, at(tx=x1), x1, ba)
    bb2 = second(1, 1, at(tx=x3), x3, bb)
    aa2 = second(0, 0, at(ty=y1), y1, aa)
    ab2 = second(0, 1, at(ty=y3), y3, ab)

    stores[0].wait()

    def hand_on(kz, gz):
        for kx in "0132":
            if kz + kx != "00":
                spread[kz + kx].wait_recv()
        return push(kcode_ref.at[gz, :, :, half, :], kcode_ref.at[gz, :, :, half, :], at(tp=q))

    k_in = [hand_on("0", z), hand_on("1", z1), hand_on("3", z3)]
    finish(1, x, vgrad_ref, (ba2, bb2))
    finish(0, y, resp_ref, (aa2, ab2))
    k_in.append(hand_on("2", z2))
    for copy in k_in:
        copy.wait_recv()
    for copy in stores[1:]:
        copy.wait()
    for copy in sends:
        copy.wait_send()


def write(resp_ref, vgrad_ref, kcode_ref, resp_out, vgrad_out, kgrad_out, cells, codes, wide, sem):
    loads = [pltpu.make_async_copy(kcode_ref.at[g], codes.at[g], sem.at[29 + g]) for g in range(4)]
    for copy in loads:
        copy.start()
    small = [
        pltpu.make_async_copy(resp_ref, cells.at[0], sem.at[33]),
        pltpu.make_async_copy(vgrad_ref, cells.at[1], sem.at[34]),
    ]
    for copy in small:
        copy.start()
    copies = [
        pltpu.make_async_copy(cells.at[0], resp_out, sem.at[27]),
        pltpu.make_async_copy(cells.at[1], vgrad_out, sem.at[28]),
    ]
    for load, copy in zip(small, copies):
        load.wait()
        copy.start()
    for n, (dz, dx, dy) in enumerate(ORDER):
        t = dz * 9 + dx * 3 + dy
        if n % 7 == 0:
            loads[n // 7].wait()
        for g in range(4):
            code = codes[n // 7, g, n % 7].astype(F32)
            unit = codes[n // 7, g, 7].astype(F32) * (1.0 / SPAN)
            wide[t, :, 128 * g : 128 * g + 128] = jnp.log(code) * unit
        copy = pltpu.make_async_copy(wide.at[t], kgrad_out.at[t], sem.at[n])
        copy.start()
        copies.append(copy)
    for copy in copies:
        copy.wait()


def shards(volume, kernel, cotangent):
    cells = 2 * 16 * 256
    scale = 1.0 / float(cells) ** 0.5
    hbm = pl.BlockSpec(memory_space=pl.ANY)
    resp, vgrad, kcode = pl.pallas_call(
        functools.partial(body, scale),
        out_shape=(
            jax.ShapeDtypeStruct((256, 128), BF16),
            jax.ShapeDtypeStruct((256, 128), BF16),
            jax.ShapeDtypeStruct((4, 4, 8, 32, 128), BF16),
        ),
        in_specs=[hbm, hbm, hbm],
        out_specs=(hbm, hbm, hbm),
        scratch_shapes=[
            pltpu.VMEM((2, 256, 128), BF16),
            pltpu.VMEM((2, 256, 128), F32),
            pltpu.VMEM((2, 2, 4, 32, 768), BF16),
            pltpu.VMEM((2, 2, 4, 32, 768), BF16),
            pltpu.VMEM((2, 256, 768), BF16),
            pltpu.VMEM((2, 256, 768), BF16),
            pltpu.VMEM((28, 4, 32, 128), BF16),
            pltpu.VMEM((28, 4, 32, 128), F32),
            pltpu.VMEM((28, 4, 16, 128), F32),
            pltpu.VMEM((3, 29, 16, 128), BF16),
            pltpu.VMEM((3, 29, 16, 128), BF16),
            pltpu.VMEM((4, 8, 16, 128), BF16),
            pltpu.VMEM((2, 2, 4, 32, 512), F32),
            pltpu.VMEM((2, 2, 2, 2, 32, 256), F32),
            pltpu.VMEM((2, 2, 2, 32, 256), F32),
            pltpu.SemaphoreType.DMA((80,)),
            pltpu.SemaphoreType.DMA((80,)),
            pltpu.SemaphoreType.DMA((7,)),
        ],
        compiler_params=pltpu.CompilerParams(
            collective_id=0, has_side_effects=True, vmem_limit_bytes=56 * 1024 * 1024
        ),
    )(volume.reshape(256, 128), cotangent.reshape(256, 128), kernel)
    resp, vgrad, kgrad = pl.pallas_call(
        write,
        out_shape=(
            jax.ShapeDtypeStruct((256, 128), BF16),
            jax.ShapeDtypeStruct((256, 128), BF16),
            jax.ShapeDtypeStruct((27, 32, 512), F32),
        ),
        in_specs=[hbm, hbm, hbm],
        out_specs=(hbm, hbm, hbm),
        scratch_shapes=[
            pltpu.VMEM((2, 256, 128), BF16),
            pltpu.VMEM((4, 4, 8, 32, 128), BF16),
            pltpu.VMEM((27, 32, 512), F32),
            pltpu.SemaphoreType.DMA((35,)),
        ],
        compiler_params=pltpu.CompilerParams(vmem_limit_bytes=56 * 1024 * 1024),
    )(resp, vgrad, kcode)
    return (resp.reshape(volume.shape), vgrad.reshape(volume.shape), kgrad)


def solution(mesh):
    in_specs = (P("ch", None, "sx", "sy"), P(None, "ch", None), P("ch", None, "sx", "sy"))
    out_specs = (P("ch", None, "sx", "sy"), P("ch", None, "sx", "sy"), P(None, "ch", None))
    return jax.shard_map(shards, mesh=mesh, in_specs=in_specs, out_specs=out_specs, check_vma=False)
```

```python
import functools

import jax
import jax.numpy as jnp
from jax import lax
from jax.experimental import pallas as pl
from jax.experimental.pallas import tpu as pltpu
from jax.sharding import PartitionSpec as P

MESH = pl.DeviceIdType.MESH
F32 = jnp.float32
BF16 = jnp.bfloat16
SPAN = 86.0
ORDER = [(dz, dx, dy) for dy in (1, 0, 2) for dz in range(3) for dx in range(3)]


def nearby(i):
    return i + 1 - 2 * (i % 2), 3 - i, (i + 2) % 4


def encode(values):
    top = jnp.max(jnp.abs(values), axis=0)
    unit = (jnp.maximum(top, 1e-30) * 1.01).astype(BF16)
    gain = SPAN / unit.astype(F32)
    return jnp.exp(values * gain[None]).astype(BF16), unit


def decode(code, unit):
    return jnp.log(code.astype(F32)) * (unit.astype(F32) * (1.0 / SPAN))[None]


class Move:
    def __init__(self, copy, may_send, may_recv):
        self.copy, self.may_send, self.may_recv = copy, may_send, may_recv
        self.when(may_send, copy.start)

    @staticmethod
    def when(may, act):
        if may is None:
            act()
        else:
            pl.when(may)(lambda: act())

    def wait_send(self):
        self.when(self.may_send, self.copy.wait_send)

    def wait_recv(self):
        self.when(self.may_recv, self.copy.wait_recv)


def body(
    scale, v_ref, c_ref, k_ref, resp_ref, vgrad_ref, kcode_ref,
    bricks, rows32, full, other, left, right, taps, kpart, kcore, rsend, rland, fin,
    part, one, two, send_sem, recv_sem, load_sem,
):
    c = lax.axis_index("ch")
    z = lax.axis_index("sx")
    p = lax.axis_index("sy")
    x, y = c // 4, c % 4
    x1, x3, x2 = nearby(x)
    y1, y3, y2 = nearby(y)
    z1, z3, z2 = nearby(z)
    up, down = (z + 1) % 4, (z + 3) % 4
    q = 1 - p

    def at(tx=None, ty=None, tz=None, tp=None):
        tx = x if tx is None else tx
        ty = y if ty is None else ty
        return {"ch": tx * 4 + ty, "sx": z if tz is None else tz, "sy": p if tp is None else tp}

    partners = [at(tx=a, tz=b) for a in (x2, x1, x3, x) for b in (z2, z1, z3, z)][:-1]
    partners += [at(ty=y2), at(ty=y1), at(ty=y3), at(tp=q)]
    barrier = pltpu.get_barrier_semaphore()
    for who in partners:
        pl.semaphore_signal(barrier, inc=1, device_id=who, device_id_type=MESH)

    half = pl.ds(pl.multiple_of(16 * p, 16), 16)
    their_half = pl.ds(pl.multiple_of(16 * q, 16), 16)
    loads = [
        pltpu.make_async_copy(v_ref, bricks.at[0], load_sem.at[0]),
        pltpu.make_async_copy(c_ref, bricks.at[1], load_sem.at[1]),
        pltpu.make_async_copy(
            k_ref.at[:, :, pl.ds(pl.multiple_of(128 * x, 128), 128)], taps.at[:, x], load_sem.at[2]
        ),
    ]
    for copy in loads:
        copy.start()

    @pl.when(z == 0)
    def _():
        full[:, :, :, :, 0:128] = jnp.zeros((2, 2, 4, 32, 128), BF16)

    @pl.when(z == 3)
    def _():
        full[:, :, :, :, 640:768] = jnp.zeros((2, 2, 4, 32, 128), BF16)

    kpart[27] = jnp.zeros((4, 32, 128), F32)

    for a, g in ((0, x), (1, y)):
        loads[a].wait()
        rows32[a] = bricks[a].astype(F32)
        for d in range(2):
            for b in range(4):
                block = rows32[a, pl.ds(d * 4 + b, 32, stride=8), :]
                full[a, d, g, :, 128 * (b + 1) : 128 * (b + 2)] = block.astype(BF16)
    pl.semaphore_wait(barrier, len(partners))

    count = [0]
    sends = []

    def push(src, dst, who, may_send=None, may_recv=None):
        n = count[0]
        count[0] += 1
        copy = pltpu.make_async_remote_copy(
            src_ref=src, dst_ref=dst, send_sem=send_sem.at[n], recv_sem=recv_sem.at[n],
            device_id=who, device_id_type=MESH,
        )
        move = Move(copy, may_send, may_recv)
        sends.append(move)
        return move

    def cells(a, g, first, n):
        return full.at[a, :, g, :, pl.ds(128 * first, 128 * n)]

    vol_in = {}
    for k, g in (("2", x2), ("1", x1), ("3", x3), ("0", x)):
        vol_in[k] = [
            push(cells(0, x, 4, 1), cells(0, x, 0, 1), at(tx=g, tz=up), z < 3, z > 0),
            push(cells(0, x, 1, 1), cells(0, x, 5, 1), at(tx=g, tz=down), z > 0, z < 3),
        ]
        if k != "0":
            vol_in[k].append(push(cells(0, x, 1, 4), cells(0, x, 1, 4), at(tx=g)))
    cot_in = [push(cells(1, y, 1, 4), cells(1, y, 1, 4), at(ty=g)) for g in (y2, y1, y3)]

    def send_taps():
        return [
            push(k_ref.at[:, half, pl.ds(pl.multiple_of(128 * g, 128), 128)], taps.at[:, x, half], at(tx=g))
            for g in (x2, x1, x3)
        ]

    tap_in = send_taps()

    cross_v = []
    for k, g in (("0", x), ("1", x1), ("3", x3), ("2", x2)):
        for copy in vol_in[k]:
            copy.wait_recv()
        cross_v.append(push(full.at[0, :, g], other.at[0, :, g], at(tp=q)))
    for copy in cot_in:
        copy.wait_recv()
    every = pl.ds(0, 4)
    cot_edges = [
        push(
            full.at[1, :, every, :, pl.ds(512, 128)], full.at[1, :, every, :, pl.ds(0, 128)], at(tz=up), z < 3, z > 0
        ),
        push(
            full.at[1, :, every, :, pl.ds(128, 128)], full.at[1, :, every, :, pl.ds(640, 128)], at(tz=down), z > 0, z < 3
        ),
    ]

    def window(a, dy, dx):
        if dy == 1:
            return full[a, :, :, :, 128 * dx : 128 * dx + 512].reshape(256, 512)
        return (left if dy == 0 else right)[a, :, 128 * dx : 128 * dx + 512]

    lane = lax.broadcasted_iota(jnp.int32, (256, 128), 1)

    def shift(a):
        for b in range(6):
            mine = full[a, :, :, :, 128 * b : 128 * b + 128].reshape(256, 128).astype(F32)
            theirs = other[a, :, :, :, 128 * b : 128 * b + 128].reshape(256, 128).astype(F32)
            before = jnp.where(lane == 127, jnp.where(p == 1, theirs, 0.0), mine)
            after = jnp.where(lane == 0, jnp.where(p == 0, theirs, 0.0), mine)
            left[a, :, 128 * b : 128 * b + 128] = pltpu.roll(before, 1, 1).astype(BF16)
            right[a, :, 128 * b : 128 * b + 128] = pltpu.roll(after, 127, 1).astype(BF16)

    cot = full[1, :, :, :, 128:640].reshape(256, 512)
    core_in = []
    for s, dy in enumerate((1, 0, 2)):
        if s == 1:
            for copy in cross_v:
                copy.wait_recv()
            shift(0)
        for dx in range(3):
            r = lax.dot_general(window(0, dy, dx), cot, (((1,), (1,)), ((), ())), preferred_element_type=F32)
            kpart[9 * s + dx] = r[:128, 128:].reshape(4, 32, 128)
            kpart[9 * s + 3 + dx] = (r[:128, :128] + r[128:, 128:]).reshape(4, 32, 128)
            kpart[9 * s + 6 + dx] = r[128:, :128].reshape(4, 32, 128)
        span = pl.ds(9 * s, 9 if s < 2 else 10)
        core_in.append(push(kpart.at[span, :, their_half], kcore.at[span], at(tp=q)))

    def cross_taps():
        moves = []
        for copy, g in zip(tap_in, (x2, x1, x3)):
            copy.wait_recv()
            moves.append(push(taps.at[:, g, half], taps.at[:, g, half], at(tp=q)))
        return moves

    tap_core = cross_taps()

    for copy in core_in:
        copy.wait_recv()
    z_in = []
    for n, g in enumerate((z2, z1, z3)):
        span = pl.ds(7 * g, 7)
        total = (kcore[span] + kpart[span, :, half, :]).reshape(28, 16, 128)
        code, unit = encode(total)
        rsend[n, 0:28] = code
        rsend[n, 28] = unit
        z_in.append(push(rsend.at[n], rland.at[n], at(tz=g)))

    for copy in cot_edges:
        copy.wait_recv()
    cross_c = push(full.at[1], other.at[1], at(tp=q))

    def filt(dx, dy):
        t = dx * 3 + dy
        w0 = taps[t].reshape(128, 128)
        w1 = taps[9 + t].reshape(128, 128)
        w2 = taps[18 + t].reshape(128, 128)
        return jnp.concatenate([jnp.concatenate([w1, w0], 1), jnp.concatenate([w2, w1], 1)], 0)

    def first(a, h, to, g1, g2):
        cut = pl.ds(256 * h, 256)
        a0 = push(part.at[a, :, g1, :, cut], one.at[a, h, 0], to)
        a1 = push(part.at[a, :, g2, :, cut], one.at[a, h, 1], to)
        return a0, a1

    def response():
        acc = jnp.zeros((256, 512), F32)
        for dx in range(3):
            for dy in range(3):
                acc += lax.dot_general(
                    filt(dx, dy), window(0, dy, dx), (((0,), (0,)), ((), ())), preferred_element_type=F32
                )
        part[0] = acc.reshape(2, 4, 32, 512)
        return first(0, 0, at(ty=y3), y3, y2), first(0, 1, at(ty=y1), y1, y2)

    def volume_gradient():
        cross_c.wait_recv()
        shift(1)
        acc = jnp.zeros((256, 512), F32)
        for dx in range(3):
            for dy in range(3):
                acc += jnp.dot(filt(dx, dy), window(1, 2 - dy, 2 - dx), preferred_element_type=F32)
        part[1] = acc.reshape(2, 4, 32, 512)
        return first(1, 0, at(tx=x3), x3, x2), first(1, 1, at(tx=x1), x1, x2)

    def second(a, h, to, g, copies):
        for copy in copies:
            copy.wait_recv()
        one[a, h, 1] += part[a, :, g, :, 256 * h : 256 * h + 256]
        return push(one.at[a, h, 1], two.at[a, h], to)

    for copy in loads[2:]:
        copy.wait()
    for copy in tap_core:
        copy.wait_recv()
    aa, ab = response()
    ba, bb = volume_gradient()

    for copy in z_in:
        copy.wait_recv()
    mine = pl.ds(7 * z, 7)
    total = (kcore[mine] + kpart[mine, :, half, :]).reshape(28, 16, 128)
    for n in range(3):
        total = total + decode(rland[n, 0:28], rland[n, 28])
    total = (total * scale).reshape(7, 4, 16, 128)
    for g in range(4):
        code, unit = encode(total[:, g])
        fin[g, 0:7] = code
        fin[g, 7] = unit
    spread = {}
    for kz, gz in (("2", z2), ("1", z1), ("3", z3), ("0", z)):
        for kx, gx in (("2", x2), ("1", x1), ("3", x3), ("0", x)):
            if kz + kx != "00":
                there = kcode_ref.at[z, x, :, half, :]
                spread[kz + kx] = push(fin.at[gx], there, at(tx=gx, tz=gz))
    kcode_ref[z, x, :, half, :] = fin[pl.ds(x, 1)].reshape(8, 16, 128)


    def finish(a, g, out_ref, copies):
        for h, copy in enumerate(copies):
            copy.wait_recv()
            for d in range(2):
                total = part[a, d, pl.ds(g, 1), :, 256 * h : 256 * h + 256].reshape(32, 256) + one[a, h, 0, d] + two[a, h, d]
                for b in range(2):
                    rows32[a, pl.ds(d * 4 + 2 * h + b, 32, stride=8), :] = total[:, 128 * b : 128 * b + 128]
        out_ref[...] = rows32[a].astype(BF16)

    aa2, ab2 = second(0, 0, at(ty=y1), y1, aa), second(0, 1, at(ty=y3), y3, ab)
    ba2, bb2 = second(1, 0, at(tx=x1), x1, ba), second(1, 1, at(tx=x3), x3, bb)

    def hand_on(kz, gz):
        for kx in "0132":
            if kz + kx != "00":
                spread[kz + kx].wait_recv()
        return push(kcode_ref.at[gz, :, :, half, :], kcode_ref.at[gz, :, :, half, :], at(tp=q))

    k_in = [hand_on("0", z)]
    k_in += [hand_on("1", z1), hand_on("3", z3)]
    finish(0, y, resp_ref, (aa2, ab2))
    finish(1, x, vgrad_ref, (ba2, bb2))
    k_in.append(hand_on("2", z2))
    for copy in k_in:
        copy.wait_recv()
    for copy in sends:
        copy.wait_send()


def write(resp_ref, vgrad_ref, kcode_ref, resp_out, vgrad_out, kgrad_out, wide, sem):
    copies = [
        pltpu.make_async_copy(resp_ref, resp_out, sem.at[27]),
        pltpu.make_async_copy(vgrad_ref, vgrad_out, sem.at[28]),
    ]
    for copy in copies:
        copy.start()
    for n, (dz, dx, dy) in enumerate(ORDER):
        t = dz * 9 + dx * 3 + dy
        for g in range(4):
            code = kcode_ref[n // 7, g, n % 7].astype(F32)
            unit = kcode_ref[n // 7, g, 7].astype(F32) * (1.0 / SPAN)
            wide[t, :, 128 * g : 128 * g + 128] = jnp.log(code) * unit
        copy = pltpu.make_async_copy(wide.at[t], kgrad_out.at[t], sem.at[n])
        copy.start()
        copies.append(copy)
    for copy in copies:
        copy.wait()


def shards(volume, kernel, cotangent):
    cells = 2 * 16 * 256
    scale = 1.0 / float(cells) ** 0.5
    vmem = pl.BlockSpec(memory_space=pltpu.VMEM)
    hbm = pl.BlockSpec(memory_space=pl.ANY)
    operands = (volume.reshape(256, 128), cotangent.reshape(256, 128), kernel)
    resp, vgrad, kcode = pl.pallas_call(
        functools.partial(body, scale),
        out_shape=(
            jax.ShapeDtypeStruct((256, 128), BF16),
            jax.ShapeDtypeStruct((256, 128), BF16),
            jax.ShapeDtypeStruct((4, 4, 8, 32, 128), BF16),
        ),
        in_specs=[hbm, hbm, hbm],
        out_specs=(vmem, vmem, vmem),
        scratch_shapes=[
            pltpu.VMEM((2, 256, 128), BF16),
            pltpu.VMEM((2, 256, 128), F32),
            pltpu.VMEM((2, 2, 4, 32, 768), BF16),
            pltpu.VMEM((2, 2, 4, 32, 768), BF16),
            pltpu.VMEM((2, 256, 768), BF16),
            pltpu.VMEM((2, 256, 768), BF16),
            pltpu.VMEM((27, 4, 32, 128), BF16),
            pltpu.VMEM((28, 4, 32, 128), F32),
            pltpu.VMEM((28, 4, 16, 128), F32),
            pltpu.VMEM((3, 29, 16, 128), BF16),
            pltpu.VMEM((3, 29, 16, 128), BF16),
            pltpu.VMEM((4, 8, 16, 128), BF16),
            pltpu.VMEM((2, 2, 4, 32, 512), F32),
            pltpu.VMEM((2, 2, 2, 2, 32, 256), F32),
            pltpu.VMEM((2, 2, 2, 32, 256), F32),
            pltpu.SemaphoreType.DMA((80,)),
            pltpu.SemaphoreType.DMA((80,)),
            pltpu.SemaphoreType.DMA((3,)),
        ],
        compiler_params=pltpu.CompilerParams(
            collective_id=0, has_side_effects=True, vmem_limit_bytes=40 * 1024 * 1024
        ),
    )(*(pltpu.with_memory_space_constraint(a, pltpu.HBM) for a in operands))
    resp, vgrad, kgrad = pl.pallas_call(
        write,
        out_shape=(
            jax.ShapeDtypeStruct((256, 128), BF16),
            jax.ShapeDtypeStruct((256, 128), BF16),
            jax.ShapeDtypeStruct((27, 32, 512), F32),
        ),
        in_specs=[vmem, vmem, vmem],
        out_specs=(hbm, hbm, hbm),
        scratch_shapes=[pltpu.VMEM((27, 32, 512), F32), pltpu.SemaphoreType.DMA((29,))],
        compiler_params=pltpu.CompilerParams(vmem_limit_bytes=40 * 1024 * 1024),
    )(resp, vgrad, kcode)
    return (resp.reshape(volume.shape), vgrad.reshape(volume.shape), kgrad)


def solution(mesh):
    in_specs = (P("ch", None, "sx", "sy"), P(None, "ch", None), P("ch", None, "sx", "sy"))
    out_specs = (P("ch", None, "sx", "sy"), P("ch", None, "sx", "sy"), P(None, "ch", None))
    return jax.shard_map(shards, mesh=mesh, in_specs=in_specs, out_specs=out_specs, check_vma=False)
```

```python
import functools

import jax
import jax.numpy as jnp
from jax import lax
from jax.experimental import pallas as pl
from jax.experimental.pallas import tpu as pltpu
from jax.sharding import PartitionSpec as P

MESH = pl.DeviceIdType.MESH
F32 = jnp.float32
BF16 = jnp.bfloat16
SPAN = 86.0
ORDER = [(dz, dx, dy) for dy in (1, 0, 2) for dz in range(3) for dx in range(3)]


def nearby(i):
    return i + 1 - 2 * (i % 2), 3 - i, (i + 2) % 4


def encode(values):
    top = jnp.max(jnp.abs(values), axis=0)
    unit = (jnp.maximum(top, 1e-30) * 1.01).astype(BF16)
    gain = SPAN / unit.astype(F32)
    return jnp.exp(values * gain[None]).astype(BF16), unit


def decode(code, unit):
    return jnp.log(code.astype(F32)) * (unit.astype(F32) * (1.0 / SPAN))[None]


class Move:
    def __init__(self, copy, may_send, may_recv):
        self.copy, self.may_send, self.may_recv = copy, may_send, may_recv
        self.when(may_send, copy.start)

    @staticmethod
    def when(may, act):
        if may is None:
            act()
        else:
            pl.when(may)(lambda: act())

    def wait_send(self):
        self.when(self.may_send, self.copy.wait_send)

    def wait_recv(self):
        self.when(self.may_recv, self.copy.wait_recv)


def body(
    scale, v_ref, c_ref, k_ref, resp_ref, vgrad_ref, kcode_ref,
    bricks, rows32, full, other, left, right, taps, far_left, far_right, sums, rsend, rland,
    part, one, two, send_sem, recv_sem, load_sem,
):
    c = lax.axis_index("ch")
    z = lax.axis_index("sx")
    p = lax.axis_index("sy")
    x, y = c // 4, c % 4
    x1, x3, x2 = nearby(x)
    y1, y3, y2 = nearby(y)
    z1, z3, z2 = nearby(z)
    up, down = (z + 1) % 4, (z + 3) % 4
    q = 1 - p

    def at(tx=None, ty=None, tz=None, tp=None):
        tx = x if tx is None else tx
        ty = y if ty is None else ty
        return {"ch": tx * 4 + ty, "sx": z if tz is None else tz, "sy": p if tp is None else tp}

    half = pl.ds(pl.multiple_of(16 * p, 16), 16)
    their_half = pl.ds(pl.multiple_of(16 * q, 16), 16)
    loads = [
        pltpu.make_async_copy(v_ref, bricks.at[0], load_sem.at[0]),
        pltpu.make_async_copy(c_ref, bricks.at[1], load_sem.at[1]),
        pltpu.make_async_copy(
            k_ref.at[:, :, pl.ds(pl.multiple_of(128 * x, 128), 128)], taps.at[:, x], load_sem.at[2]
        ),
    ]
    for copy in loads:
        copy.start()

    partners = [at(tx=a, tz=b) for a in (x2, x1, x3, x) for b in (z2, z1, z3, z)][:-1]
    partners += [at(ty=y2), at(ty=y1), at(ty=y3), at(tp=q)]
    barrier = pltpu.get_barrier_semaphore()
    for who in partners:
        pl.semaphore_signal(barrier, inc=1, device_id=who, device_id_type=MESH)

    @pl.when(z == 0)
    def _():
        full[:, :, :, :, 0:128] = jnp.zeros((2, 2, 4, 32, 128), BF16)

    @pl.when(z == 3)
    def _():
        full[:, :, :, :, 640:768] = jnp.zeros((2, 2, 4, 32, 128), BF16)

    sums[27] = jnp.zeros((4, 16, 128), F32)

    for a, g in ((0, x), (1, y)):
        loads[a].wait()
        rows32[a] = bricks[a].astype(F32)
        for d in range(2):
            for b in range(4):
                block = rows32[a, pl.ds(d * 4 + b, 32, stride=8), :]
                full[a, d, g, :, 128 * (b + 1) : 128 * (b + 2)] = block.astype(BF16)
    pl.semaphore_wait(barrier, len(partners))

    count = [0]
    sends = []

    def push(src, dst, who, may_send=None, may_recv=None):
        n = count[0]
        count[0] += 1
        copy = pltpu.make_async_remote_copy(
            src_ref=src, dst_ref=dst, send_sem=send_sem.at[n], recv_sem=recv_sem.at[n],
            device_id=who, device_id_type=MESH,
        )
        move = Move(copy, may_send, may_recv)
        sends.append(move)
        return move

    def cells(a, g, first, n):
        return full.at[a, :, g, :, pl.ds(128 * first, 128 * n)]

    vol_in = {}
    for k, g in (("2", x2), ("1", x1), ("3", x3), ("0", x)):
        vol_in[k] = [
            push(cells(0, x, 4, 1), cells(0, x, 0, 1), at(tx=g, tz=up), z < 3, z > 0),
            push(cells(0, x, 1, 1), cells(0, x, 5, 1), at(tx=g, tz=down), z > 0, z < 3),
        ]
        if k != "0":
            vol_in[k].append(push(cells(0, x, 1, 4), cells(0, x, 1, 4), at(tx=g)))
    cot_in = [push(cells(1, y, 1, 4), cells(1, y, 1, 4), at(ty=g)) for g in (y1, y3, y2)]

    def send_taps():
        return [
            push(k_ref.at[:, half, pl.ds(pl.multiple_of(128 * g, 128), 128)], taps.at[:, x, half], at(tx=g))
            for g in (x2, x1, x3)
        ]


    cross_v = {}

    def arrive(k, g):
        for copy in vol_in[k]:
            copy.wait_recv()
        cross_v[k] = push(full.at[0, :, g], other.at[0, :, g], at(tp=q))

    cross_c = [push(cells(1, y, 1, 4), other.at[1, :, y, :, pl.ds(128, 512)], at(tp=q))]
    arrive("0", x)
    arrive("1", x1)
    tap_in = send_taps()
    for copy, g in zip(cot_in, (y1, y3, y2)):
        copy.wait_recv()
        cross_c.append(push(cells(1, g, 1, 4), other.at[1, :, g, :, pl.ds(128, 512)], at(tp=q)))
    arrive("3", x3)
    arrive("2", x2)
    every = pl.ds(0, 4)
    low, high = pl.ds(0, 128), pl.ds(640, 128)
    cot_edges = [
        push(full.at[1, :, every, :, pl.ds(512, 128)], full.at[1, :, every, :, low], at(tz=up), z < 3, z > 0),
        push(full.at[1, :, every, :, pl.ds(128, 128)], full.at[1, :, every, :, high], at(tz=down), z > 0, z < 3),
    ]

    def window(a, dy, dx):
        ref = full if dy == 1 else left if dy == 0 else right
        return ref[a, :, :, :, 128 * dx : 128 * dx + 512].reshape(256, 512)

    def shift(near, far, side, place):
        for b in range(6):
            mine = near[:, place[0], place[1], 128 * b : 128 * b + 128].astype(F32)
            theirs = far[:, place[0], place[1], 128 * b : 128 * b + 128].astype(F32)
            lane = lax.broadcasted_iota(jnp.int32, mine.shape, 3)
            before = jnp.where(lane == 127, jnp.where(side == 1, theirs, 0.0), mine)
            after = jnp.where(lane == 0, jnp.where(side == 0, theirs, 0.0), mine)
            flat = (mine.size // 128, 128)
            before = pltpu.roll(before.reshape(flat), 1, 1).astype(BF16).reshape(mine.shape)
            after = pltpu.roll(after.reshape(flat), 127, 1).astype(BF16).reshape(mine.shape)
            yield b, before, after

    bases = (2 * (x // 2), 2 * (1 - x // 2))

    def brick_gradient(h):
        pair = pl.ds(bases[h], 2)
        for b, before, after in shift(full.at[0], other.at[0], p, (pair, half)):
            left[0, :, pair, half, 128 * b : 128 * b + 128] = before
            right[0, :, pair, half, 128 * b : 128 * b + 128] = after
        for b, before, after in shift(other.at[0], full.at[0], q, (pair, half)):
            far_left[:, :, :, 128 * b : 128 * b + 128] = before
            far_right[:, :, :, 128 * b : 128 * b + 128] = after
        total = None
        for refs, cots in (
            ((full.at[0, :, pair, half], left.at[0, :, pair, half], right.at[0, :, pair, half]), full),
            ((other.at[0, :, pair, half], far_left, far_right), other),
        ):
            cot = cots[1, :, :, :, 128:640].reshape(256, 512)
            stack = [
                refs[at_y][:, :, :, 128 * dx : 128 * dx + 512].reshape(64, 512) for at_y in range(3) for dx in range(3)
            ]
            r = lax.dot_general(
                jnp.concatenate(stack, 0), cot, (((1,), (1,)), ((), ())), preferred_element_type=F32
            )
            total = r if total is None else total + r
        for s in range(3):
            for dx in range(3):
                r = total[64 * (3 * s + dx) : 64 * (3 * s + dx) + 64]
                sums[9 * s + dx, pair] = r[:32, 128:].reshape(2, 16, 128)
                sums[9 * s + 3 + dx, pair] = (r[:32, :128] + r[32:, 128:]).reshape(2, 16, 128)
                sums[9 * s + 6 + dx, pair] = r[32:, :128].reshape(2, 16, 128)

    x_places = ((("1", x1), ("0", x)), (("2", x2), ("3", x3)))
    z_places = (("2", z2), ("1", z1), ("3", z3), ("0", z))
    z_in = ({}, {})

    def send_sums(h):
        pair = pl.ds(bases[h], 2)
        for n, (kz, gz) in enumerate(z_places):
            code, unit = encode(sums[pl.ds(7 * gz, 7), pair])
            for g in range(2):
                rsend[h, n, g, 0:7] = code[:, g]
                rsend[h, n, g, 7] = unit[g]
            for m, (kx, gx) in enumerate(x_places[h]):
                if kz + kx != "00":
                    z_in[h][kz + kx] = push(rsend.at[h, n, gx % 2], rland.at[h, n, m], at(tx=gx, tz=gz))

    for copy in cross_c:
        copy.wait_recv()
    cross_v["0"].wait_recv()
    cross_v["1"].wait_recv()
    brick_gradient(0)
    send_sums(0)
    cross_v["3"].wait_recv()
    cross_v["2"].wait_recv()
    brick_gradient(1)
    send_sums(1)

    def cross_taps():
        moves = []
        for copy, g in zip(tap_in, (x2, x1, x3)):
            copy.wait_recv()
            moves.append(push(taps.at[:, g, half], taps.at[:, g, half], at(tp=q)))
        return moves

    tap_core = cross_taps()

    for copy in cot_edges:
        copy.wait_recv()
    cross_e = [push(full.at[1, :, every, :, side], other.at[1, :, every, :, side], at(tp=q)) for side in (low, high)]

    def filt(dx, dy):
        t = dx * 3 + dy
        w0 = taps[t].reshape(128, 128)
        w1 = taps[9 + t].reshape(128, 128)
        w2 = taps[18 + t].reshape(128, 128)
        return jnp.concatenate([jnp.concatenate([w1, w0], 1), jnp.concatenate([w2, w1], 1)], 0)

    def first(a, h, to, g1, g2):
        cut = pl.ds(256 * h, 256)
        a0 = push(part.at[a, :, g1, :, cut], one.at[a, h, 0], to)
        a1 = push(part.at[a, :, g2, :, cut], one.at[a, h, 1], to)
        return a0, a1

    def response():
        for b, before, after in shift(full.at[0], other.at[0], p, (every, their_half)):
            left[0, :, :, their_half, 128 * b : 128 * b + 128] = before
            right[0, :, :, their_half, 128 * b : 128 * b + 128] = after
        acc = jnp.zeros((256, 512), F32)
        for dx in range(3):
            for dy in range(3):
                acc += lax.dot_general(
                    filt(dx, dy), window(0, dy, dx), (((0,), (0,)), ((), ())), preferred_element_type=F32
                )
        part[0] = acc.reshape(2, 4, 32, 512)
        return first(0, 0, at(ty=y3), y3, y2), first(0, 1, at(ty=y1), y1, y2)

    def volume_gradient():
        for copy in cross_e:
            copy.wait_recv()
        for b, before, after in shift(full.at[1], other.at[1], p, (every, pl.ds(0, 32))):
            left[1, :, :, :, 128 * b : 128 * b + 128] = before
            right[1, :, :, :, 128 * b : 128 * b + 128] = after
        acc = jnp.zeros((256, 512), F32)
        for dx in range(3):
            for dy in range(3):
                acc += jnp.dot(filt(dx, dy), window(1, 2 - dy, 2 - dx), preferred_element_type=F32)
        part[1] = acc.reshape(2, 4, 32, 512)
        return first(1, 0, at(tx=x3), x3, x2), first(1, 1, at(tx=x1), x1, x2)

    def second(a, h, to, g, copies):
        for copy in copies:
            copy.wait_recv()
        one[a, h, 1] += part[a, :, g, :, 256 * h : 256 * h + 256]
        return push(one.at[a, h, 1], two.at[a, h], to)

    for copy in loads[2:]:
        copy.wait()
    for copy in tap_core:
        copy.wait_recv()
    aa, ab = response()
    ba, bb = volume_gradient()

    mine = pl.ds(7 * z, 7)
    k_z, k_in = ({}, {}), []

    def send_result(h):
        for copy in z_in[h].values():
            copy.wait_recv()
        for m, (kx, gx) in enumerate(x_places[h]):
            total = jnp.zeros((7, 16, 128), F32)
            for n, (kz, gz) in enumerate(z_places):
                if kz + kx == "00":
                    total = total + sums[mine, pl.ds(x, 1)].reshape(7, 16, 128)
                else:
                    total = total + decode(rland[h, n, m, 0:7], rland[h, n, m, 7])
            code, unit = encode(total * scale)
            kcode_ref[z, gx, 0:7, half, :] = code
            kcode_ref[z, gx, 7, half, :] = unit
        there = kcode_ref.at[z, pl.ds(bases[h], 2), :, half, :]
        for kz, gz in z_places[:3]:
            k_z[h][kz] = push(there, there, at(tz=gz))
        k_in.append(push(there, there, at(tp=q)))

    send_result(0)
    send_result(1)
    aa2, ab2 = second(0, 0, at(ty=y1), y1, aa), second(0, 1, at(ty=y3), y3, ab)
    ba2, bb2 = second(1, 0, at(tx=x1), x1, ba), second(1, 1, at(tx=x3), x3, bb)

    def finish(a, g, out_ref, copies):
        for h, copy in enumerate(copies):
            copy.wait_recv()
            for d in range(2):
                total = part[a, d, pl.ds(g, 1), :, 256 * h : 256 * h + 256].reshape(32, 256) + one[a, h, 0, d] + two[a, h, d]
                for b in range(2):
                    rows32[a, pl.ds(d * 4 + 2 * h + b, 32, stride=8), :] = total[:, 128 * b : 128 * b + 128]
        out_ref[...] = rows32[a].astype(BF16)


    def hand_on(h, kz, gz):
        k_z[h][kz].wait_recv()
        there = kcode_ref.at[gz, pl.ds(bases[h], 2), :, half, :]
        k_in.append(push(there, there, at(tp=q)))

    for h, kz, gz in ((0, "1", z1), (0, "3", z3), (0, "2", z2)):
        hand_on(h, kz, gz)
    hand_on(1, "1", z1)
    hand_on(1, "3", z3)
    finish(0, y, resp_ref, (aa2, ab2))
    finish(1, x, vgrad_ref, (ba2, bb2))
    hand_on(1, "2", z2)
    for copy in k_in:
        copy.wait_recv()
    for copy in sends:
        copy.wait_send()


def write(resp_ref, vgrad_ref, kcode_ref, resp_out, vgrad_out, kgrad_out, wide, sem):
    copies = [
        pltpu.make_async_copy(resp_ref, resp_out, sem.at[27]),
        pltpu.make_async_copy(vgrad_ref, vgrad_out, sem.at[28]),
    ]
    for copy in copies:
        copy.start()
    for n, (dz, dx, dy) in enumerate(ORDER):
        t = dz * 9 + dx * 3 + dy
        for g in range(4):
            code = kcode_ref[n // 7, g, n % 7].astype(F32)
            unit = kcode_ref[n // 7, g, 7].astype(F32) * (1.0 / SPAN)
            wide[t, :, 128 * g : 128 * g + 128] = jnp.log(code) * unit
        copy = pltpu.make_async_copy(wide.at[t], kgrad_out.at[t], sem.at[n])
        copy.start()
        copies.append(copy)
    for copy in copies:
        copy.wait()


def shards(volume, kernel, cotangent):
    cells = 2 * 16 * 256
    scale = 1.0 / float(cells) ** 0.5
    vmem = pl.BlockSpec(memory_space=pltpu.VMEM)
    hbm = pl.BlockSpec(memory_space=pl.ANY)
    operands = (volume.reshape(256, 128), cotangent.reshape(256, 128), kernel)
    resp, vgrad, kcode = pl.pallas_call(
        functools.partial(body, scale),
        out_shape=(
            jax.ShapeDtypeStruct((256, 128), BF16),
            jax.ShapeDtypeStruct((256, 128), BF16),
            jax.ShapeDtypeStruct((4, 4, 8, 32, 128), BF16),
        ),
        in_specs=[hbm, hbm, hbm],
        out_specs=(vmem, vmem, vmem),
        scratch_shapes=[
            pltpu.VMEM((2, 256, 128), BF16),
            pltpu.VMEM((2, 256, 128), F32),
            pltpu.VMEM((2, 2, 4, 32, 768), BF16),
            pltpu.VMEM((2, 2, 4, 32, 768), BF16),
            pltpu.VMEM((2, 2, 4, 32, 768), BF16),
            pltpu.VMEM((2, 2, 4, 32, 768), BF16),
            pltpu.VMEM((27, 4, 32, 128), BF16),
            pltpu.VMEM((2, 2, 16, 768), BF16),
            pltpu.VMEM((2, 2, 16, 768), BF16),
            pltpu.VMEM((28, 4, 16, 128), F32),
            pltpu.VMEM((2, 4, 2, 8, 16, 128), BF16),
            pltpu.VMEM((2, 4, 2, 8, 16, 128), BF16),
            pltpu.VMEM((2, 2, 4, 32, 512), F32),
            pltpu.VMEM((2, 2, 2, 2, 32, 256), F32),
            pltpu.VMEM((2, 2, 2, 32, 256), F32),
            pltpu.SemaphoreType.DMA((80,)),
            pltpu.SemaphoreType.DMA((80,)),
            pltpu.SemaphoreType.DMA((3,)),
        ],
        compiler_params=pltpu.CompilerParams(
            collective_id=0, has_side_effects=True, vmem_limit_bytes=40 * 1024 * 1024
        ),
    )(*(pltpu.with_memory_space_constraint(a, pltpu.HBM) for a in operands))
    resp, vgrad, kgrad = pl.pallas_call(
        write,
        out_shape=(
            jax.ShapeDtypeStruct((256, 128), BF16),
            jax.ShapeDtypeStruct((256, 128), BF16),
            jax.ShapeDtypeStruct((27, 32, 512), F32),
        ),
        in_specs=[vmem, vmem, vmem],
        out_specs=(hbm, hbm, hbm),
        scratch_shapes=[pltpu.VMEM((27, 32, 512), F32), pltpu.SemaphoreType.DMA((29,))],
        compiler_params=pltpu.CompilerParams(vmem_limit_bytes=40 * 1024 * 1024),
    )(resp, vgrad, kcode)
    return (resp.reshape(volume.shape), vgrad.reshape(volume.shape), kgrad)


def solution(mesh):
    in_specs = (P("ch", None, "sx", "sy"), P(None, "ch", None), P("ch", None, "sx", "sy"))
    out_specs = (P("ch", None, "sx", "sy"), P("ch", None, "sx", "sy"), P(None, "ch", None))
    return jax.shard_map(shards, mesh=mesh, in_specs=in_specs, out_specs=out_specs, check_vma=False)
```

```python
import functools

import jax
import jax.numpy as jnp
from jax import lax
from jax.experimental import pallas as pl
from jax.experimental.pallas import tpu as pltpu
from jax.sharding import PartitionSpec as P

MESH = pl.DeviceIdType.MESH
F32 = jnp.float32
BF16 = jnp.bfloat16
SPAN = 86.0


def nearby(i):
    return i + 1 - 2 * (i % 2), 3 - i, (i + 2) % 4


def encode(values):
    top = jnp.max(jnp.abs(values), axis=0)
    unit = (jnp.maximum(top, 1e-30) * 1.01).astype(BF16)
    gain = SPAN / unit.astype(F32)
    return jnp.exp(values * gain[None]).astype(BF16), unit


def decode(code, unit):
    return jnp.log(code.astype(F32)) * (unit.astype(F32) * (1.0 / SPAN))[None]


class Move:
    def __init__(self, copy, may_send, may_recv):
        self.copy, self.may_send, self.may_recv = copy, may_send, may_recv
        self.when(may_send, copy.start)

    @staticmethod
    def when(may, act):
        if may is None:
            act()
        else:
            pl.when(may)(lambda: act())

    def wait_send(self):
        self.when(self.may_send, self.copy.wait_send)

    def wait_recv(self):
        self.when(self.may_recv, self.copy.wait_recv)


def body(
    scale, v_ref, c_ref, k_ref, resp_ref, vgrad_ref, kcode_ref,
    bricks, rows32, full, other, left, right, taps, far_left, far_right, sums, rsend, rland,
    part, one, two, send_sem, recv_sem, load_sem,
):
    c = lax.axis_index("ch")
    z = lax.axis_index("sx")
    p = lax.axis_index("sy")
    x, y = c // 4, c % 4
    x1, x3, x2 = nearby(x)
    y1, y3, y2 = nearby(y)
    z1, z3, z2 = nearby(z)
    up, down = (z + 1) % 4, (z + 3) % 4
    q = 1 - p

    def at(tx=None, ty=None, tz=None, tp=None):
        tx = x if tx is None else tx
        ty = y if ty is None else ty
        return {"ch": tx * 4 + ty, "sx": z if tz is None else tz, "sy": p if tp is None else tp}

    half = pl.ds(pl.multiple_of(16 * p, 16), 16)
    their_half = pl.ds(pl.multiple_of(16 * q, 16), 16)
    loads = [
        pltpu.make_async_copy(v_ref, bricks.at[0], load_sem.at[0]),
        pltpu.make_async_copy(c_ref, bricks.at[1], load_sem.at[1]),
        pltpu.make_async_copy(
            k_ref.at[:, :, pl.ds(pl.multiple_of(128 * x, 128), 128)], taps.at[:, x], load_sem.at[2]
        ),
    ]
    for copy in loads:
        copy.start()

    partners = [at(tx=a, tz=b) for a in (x2, x1, x3, x) for b in (z2, z1, z3, z)][:-1]
    partners += [at(ty=y2), at(ty=y1), at(ty=y3), at(tp=q)]
    barrier = pltpu.get_barrier_semaphore()
    for who in partners:
        pl.semaphore_signal(barrier, inc=1, device_id=who, device_id_type=MESH)

    @pl.when(z == 0)
    def _():
        full[:, :, :, :, 0:128] = jnp.zeros((2, 2, 4, 32, 128), BF16)

    @pl.when(z == 3)
    def _():
        full[:, :, :, :, 640:768] = jnp.zeros((2, 2, 4, 32, 128), BF16)

    sums[27] = jnp.zeros((4, 16, 128), F32)

    for a, g in ((0, x), (1, y)):
        loads[a].wait()
        rows32[a] = bricks[a].astype(F32)
        for d in range(2):
            for b in range(4):
                block = rows32[a, pl.ds(d * 4 + b, 32, stride=8), :]
                full[a, d, g, :, 128 * (b + 1) : 128 * (b + 2)] = block.astype(BF16)
    pl.semaphore_wait(barrier, len(partners))

    count = [0]
    sends = []

    def push(src, dst, who, may_send=None, may_recv=None):
        n = count[0]
        count[0] += 1
        copy = pltpu.make_async_remote_copy(
            src_ref=src, dst_ref=dst, send_sem=send_sem.at[n], recv_sem=recv_sem.at[n],
            device_id=who, device_id_type=MESH,
        )
        move = Move(copy, may_send, may_recv)
        sends.append(move)
        return move

    def drain(upto):
        for move in sends[:upto]:
            move.wait_send()
        del sends[:upto]

    def cells(a, g, first, n):
        return full.at[a, :, g, :, pl.ds(128 * first, 128 * n)]

    vol_in = {}
    for k, g in (("2", x2), ("1", x1), ("3", x3), ("0", x)):
        vol_in[k] = [
            push(cells(0, x, 4, 1), cells(0, x, 0, 1), at(tx=g, tz=up), z < 3, z > 0),
            push(cells(0, x, 1, 1), cells(0, x, 5, 1), at(tx=g, tz=down), z > 0, z < 3),
        ]
        if k != "0":
            vol_in[k].append(push(cells(0, x, 1, 4), cells(0, x, 1, 4), at(tx=g)))
    cot_in = [push(cells(1, y, 1, 4), cells(1, y, 1, 4), at(ty=g)) for g in (y1, y3, y2)]

    def send_taps():
        return [
            push(k_ref.at[:, half, pl.ds(pl.multiple_of(128 * g, 128), 128)], taps.at[:, x, half], at(tx=g))
            for g in (x2, x1, x3)
        ]


    cross_v = {}

    def arrive(k, g):
        for copy in vol_in[k]:
            copy.wait_recv()
        cross_v[k] = push(full.at[0, :, g], other.at[0, :, g], at(tp=q))

    cross_c = [push(cells(1, y, 1, 4), other.at[1, :, y, :, pl.ds(128, 512)], at(tp=q))]
    arrive("0", x)
    arrive("1", x1)
    tap_in = send_taps()
    for copy, g in zip(cot_in, (y1, y3, y2)):
        copy.wait_recv()
        cross_c.append(push(cells(1, g, 1, 4), other.at[1, :, g, :, pl.ds(128, 512)], at(tp=q)))
    arrive("3", x3)
    arrive("2", x2)
    every = pl.ds(0, 4)
    low, high = pl.ds(0, 128), pl.ds(640, 128)
    cot_edges = [
        push(full.at[1, :, every, :, pl.ds(512, 128)], full.at[1, :, every, :, low], at(tz=up), z < 3, z > 0),
        push(full.at[1, :, every, :, pl.ds(128, 128)], full.at[1, :, every, :, high], at(tz=down), z > 0, z < 3),
    ]

    def window(a, dy, dx):
        ref = full if dy == 1 else left if dy == 0 else right
        return ref[a, :, :, :, 128 * dx : 128 * dx + 512].reshape(256, 512)

    def shift(near, far, side, place):
        for b in range(6):
            mine = near[:, place[0], place[1], 128 * b : 128 * b + 128].astype(F32)
            theirs = far[:, place[0], place[1], 128 * b : 128 * b + 128].astype(F32)
            lane = lax.broadcasted_iota(jnp.int32, mine.shape, mine.ndim - 1)
            before = jnp.where(lane == 127, jnp.where(side == 1, theirs, 0.0), mine)
            after = jnp.where(lane == 0, jnp.where(side == 0, theirs, 0.0), mine)
            flat = (mine.size // 128, 128)
            before = pltpu.roll(before.reshape(flat), 1, 1).astype(BF16).reshape(mine.shape)
            after = pltpu.roll(after.reshape(flat), 127, 1).astype(BF16).reshape(mine.shape)
            yield b, before, after

    x_places = ((("0", x), ("1", x1)), (("3", x3), ("2", x2)))
    z_places = (("2", z2), ("1", z1), ("3", z3), ("0", z))

    def brick_gradient(h):
        total = None
        views = []
        for m, (kx, g) in enumerate(x_places[h]):
            for b, before, after in shift(full.at[0], other.at[0], p, (g, half)):
                left[0, :, g, half, 128 * b : 128 * b + 128] = before
                right[0, :, g, half, 128 * b : 128 * b + 128] = after
            for b, before, after in shift(other.at[0], full.at[0], q, (g, half)):
                far_left[m, :, :, 128 * b : 128 * b + 128] = before
                far_right[m, :, :, 128 * b : 128 * b + 128] = after
            views.append((
                (full.at[0, :, g, half], left.at[0, :, g, half], right.at[0, :, g, half]),
                (other.at[0, :, g, half], far_left.at[m], far_right.at[m]),
            ))
        for brick, cots in ((0, full), (1, other)):
            cot = cots[1, :, :, :, 128:640].reshape(256, 512)
            stack = [
                views[m][brick][s][:, :, 128 * dx : 128 * dx + 512].reshape(32, 512)
                for s in range(3) for dx in range(3) for m in range(2)
            ]
            r = lax.dot_general(
                jnp.concatenate(stack, 0), cot, (((1,), (1,)), ((), ())), preferred_element_type=F32
            )
            total = r if total is None else total + r
        for s in range(3):
            for dx in range(3):
                for m, (kx, g) in enumerate(x_places[h]):
                    at_row = 32 * (6 * s + 2 * dx + m)
                    r = total[at_row : at_row + 32]
                    tap = 3 * dx + (1, 0, 2)[s]
                    sums[tap, g] = r[:16, 128:]
                    sums[9 + tap, g] = r[:16, :128] + r[16:, 128:]
                    sums[18 + tap, g] = r[16:, :128]

    z_in = ({}, {})

    def send_sums(h):
        for n, (kz, gz) in enumerate(z_places):
            for m, (kx, gx) in enumerate(x_places[h]):
                if kz + kx != "00":
                    code, unit = encode(sums[pl.ds(7 * gz, 7), pl.ds(gx, 1)].reshape(7, 16, 128))
                    rsend[h, n, m, 0:7] = code
                    rsend[h, n, m, 7] = unit
                    z_in[h][kz + kx] = push(rsend.at[h, n, m], rland.at[h, n, m], at(tx=gx, tz=gz))

    for copy in cross_c:
        copy.wait_recv()
    for h in range(2):
        for kx, g in x_places[h]:
            cross_v[kx].wait_recv()
        brick_gradient(h)
        send_sums(h)

    def cross_taps():
        moves = []
        for copy, g in zip(tap_in, (x2, x1, x3)):
            copy.wait_recv()
            moves.append(push(taps.at[:, g, half], taps.at[:, g, half], at(tp=q)))
        return moves

    tap_core = cross_taps()

    for copy in cot_edges:
        copy.wait_recv()
    cross_e = [push(full.at[1, :, every, :, side], other.at[1, :, every, :, side], at(tp=q)) for side in (low, high)]

    def filt(dx, dy):
        t = dx * 3 + dy
        w0 = taps[t].reshape(128, 128)
        w1 = taps[9 + t].reshape(128, 128)
        w2 = taps[18 + t].reshape(128, 128)
        return jnp.concatenate([jnp.concatenate([w1, w0], 1), jnp.concatenate([w2, w1], 1)], 0)

    def first(a, h, to, g1, g2):
        cut = pl.ds(256 * h, 256)
        a0 = push(part.at[a, :, g1, :, cut], one.at[a, h, 0], to)
        a1 = push(part.at[a, :, g2, :, cut], one.at[a, h, 1], to)
        return a0, a1

    def response():
        for b, before, after in shift(full.at[0], other.at[0], p, (every, their_half)):
            left[0, :, :, their_half, 128 * b : 128 * b + 128] = before
            right[0, :, :, their_half, 128 * b : 128 * b + 128] = after
        acc = jnp.zeros((256, 512), F32)
        for dx in range(3):
            for dy in range(3):
                acc += lax.dot_general(
                    filt(dx, dy), window(0, dy, dx), (((0,), (0,)), ((), ())), preferred_element_type=F32
                )
        part[0] = acc.reshape(2, 4, 32, 512)
        return first(0, 0, at(ty=y3), y3, y2), first(0, 1, at(ty=y1), y1, y2)

    def volume_gradient():
        for copy in cross_e:
            copy.wait_recv()
        for b, before, after in shift(full.at[1], other.at[1], p, (every, pl.ds(0, 32))):
            left[1, :, :, :, 128 * b : 128 * b + 128] = before
            right[1, :, :, :, 128 * b : 128 * b + 128] = after
        acc = jnp.zeros((256, 512), F32)
        for dx in range(3):
            for dy in range(3):
                acc += jnp.dot(filt(dx, dy), window(1, 2 - dy, 2 - dx), preferred_element_type=F32)
        part[1] = acc.reshape(2, 4, 32, 512)
        return first(1, 0, at(tx=x3), x3, x2), first(1, 1, at(tx=x1), x1, x2)

    def second(a, h, to, g, copies):
        for copy in copies:
            copy.wait_recv()
        one[a, h, 1] += part[a, :, g, :, 256 * h : 256 * h + 256]
        return push(one.at[a, h, 1], two.at[a, h], to)

    for copy in loads[2:]:
        copy.wait()
    for copy in tap_core:
        copy.wait_recv()
    early = len(sends)
    aa, ab = response()
    ba, bb = volume_gradient()
    drain(early)

    mine = pl.ds(7 * z, 7)
    k_z, k_in = ({}, {}), []

    def send_result(h):
        for copy in z_in[h].values():
            copy.wait_recv()
        for m, (kx, gx) in enumerate(x_places[h]):
            total = jnp.zeros((7, 16, 128), F32)
            for n, (kz, gz) in enumerate(z_places):
                if kz + kx == "00":
                    total = total + sums[mine, pl.ds(x, 1)].reshape(7, 16, 128)
                else:
                    total = total + decode(rland[h, n, m, 0:7], rland[h, n, m, 7])
            code, unit = encode(total * scale)
            kcode_ref[z, h, m, 0:7, half, :] = code
            kcode_ref[z, h, m, 7, half, :] = unit
        there = kcode_ref.at[z, h, :, :, half, :]
        for kz, gz in z_places[:3]:
            k_z[h][kz] = push(there, there, at(tz=gz))
        k_in.append(push(there, there, at(tp=q)))

    send_result(0)
    send_result(1)
    aa2, ab2 = second(0, 0, at(ty=y1), y1, aa), second(0, 1, at(ty=y3), y3, ab)
    ba2, bb2 = second(1, 0, at(tx=x1), x1, ba), second(1, 1, at(tx=x3), x3, bb)

    def finish(a, g, out_ref, copies):
        for h, copy in enumerate(copies):
            copy.wait_recv()
            for d in range(2):
                total = part[a, d, pl.ds(g, 1), :, 256 * h : 256 * h + 256].reshape(32, 256) + one[a, h, 0, d] + two[a, h, d]
                for b in range(2):
                    rows32[a, pl.ds(d * 4 + 2 * h + b, 32, stride=8), :] = total[:, 128 * b : 128 * b + 128]
        out_ref[...] = rows32[a].astype(BF16)


    drain(len(sends) - 12)

    def hand_on(h, kz, gz):
        k_z[h][kz].wait_recv()
        there = kcode_ref.at[gz, h, :, :, half, :]
        k_in.append(push(there, there, at(tp=q)))

    for h, kz, gz in ((0, "1", z1), (0, "3", z3), (0, "2", z2)):
        hand_on(h, kz, gz)
    hand_on(1, "1", z1)
    hand_on(1, "3", z3)
    finish(0, y, resp_ref, (aa2, ab2))
    hand_on(1, "2", z2)
    finish(1, x, vgrad_ref, (ba2, bb2))
    for copy in k_in:
        copy.wait_recv()
    for copy in sends:
        copy.wait_send()


def write(resp_ref, vgrad_ref, kcode_ref, resp_out, vgrad_out, kgrad_out, wide, sem):
    copies = [
        pltpu.make_async_copy(resp_ref, resp_out, sem.at[27]),
        pltpu.make_async_copy(vgrad_ref, vgrad_out, sem.at[28]),
    ]
    for copy in copies:
        copy.start()
    x = lax.axis_index("ch") // 4
    x1, x3, x2 = nearby(x)
    places = (x, x1, x3, x2)
    for t in range(27):
        for k, g in enumerate(places):
            code = kcode_ref[t // 7, k // 2, k % 2, t % 7].astype(F32)
            unit = kcode_ref[t // 7, k // 2, k % 2, 7].astype(F32) * (1.0 / SPAN)
            wide[t, :, pl.ds(pl.multiple_of(128 * g, 128), 128)] = jnp.log(code) * unit
        if t % 1 == 0:
            span = pl.ds(t - 0, 1)
            copies.append(pltpu.make_async_copy(wide.at[span], kgrad_out.at[span], sem.at[t]))
            copies[-1].start()
    for copy in copies:
        copy.wait()


def shards(volume, kernel, cotangent):
    cells = 2 * 16 * 256
    scale = 1.0 / float(cells) ** 0.5
    vmem = pl.BlockSpec(memory_space=pltpu.VMEM)
    hbm = pl.BlockSpec(memory_space=pl.ANY)
    operands = (volume.reshape(256, 128), cotangent.reshape(256, 128), kernel)
    resp, vgrad, kcode = pl.pallas_call(
        functools.partial(body, scale),
        out_shape=(
            jax.ShapeDtypeStruct((256, 128), BF16),
            jax.ShapeDtypeStruct((256, 128), BF16),
            jax.ShapeDtypeStruct((4, 2, 2, 8, 32, 128), BF16),
        ),
        in_specs=[hbm, hbm, hbm],
        out_specs=(vmem, vmem, vmem),
        scratch_shapes=[
            pltpu.VMEM((2, 256, 128), BF16),
            pltpu.VMEM((2, 256, 128), F32),
            pltpu.VMEM((2, 2, 4, 32, 768), BF16),
            pltpu.VMEM((2, 2, 4, 32, 768), BF16),
            pltpu.VMEM((2, 2, 4, 32, 768), BF16),
            pltpu.VMEM((2, 2, 4, 32, 768), BF16),
            pltpu.VMEM((27, 4, 32, 128), BF16),
            pltpu.VMEM((2, 2, 16, 768), BF16),
            pltpu.VMEM((2, 2, 16, 768), BF16),
            pltpu.VMEM((28, 4, 16, 128), F32),
            pltpu.VMEM((2, 4, 2, 8, 16, 128), BF16),
            pltpu.VMEM((2, 4, 2, 8, 16, 128), BF16),
            pltpu.VMEM((2, 2, 4, 32, 512), F32),
            pltpu.VMEM((2, 2, 2, 2, 32, 256), F32),
            pltpu.VMEM((2, 2, 2, 32, 256), F32),
            pltpu.SemaphoreType.DMA((80,)),
            pltpu.SemaphoreType.DMA((80,)),
            pltpu.SemaphoreType.DMA((3,)),
        ],
        compiler_params=pltpu.CompilerParams(
            collective_id=0, has_side_effects=True, vmem_limit_bytes=40 * 1024 * 1024
        ),
    )(*(pltpu.with_memory_space_constraint(a, pltpu.HBM) for a in operands))
    resp, vgrad, kgrad = pl.pallas_call(
        write,
        out_shape=(
            jax.ShapeDtypeStruct((256, 128), BF16),
            jax.ShapeDtypeStruct((256, 128), BF16),
            jax.ShapeDtypeStruct((27, 32, 512), F32),
        ),
        in_specs=[vmem, vmem, vmem],
        out_specs=(hbm, hbm, hbm),
        scratch_shapes=[pltpu.VMEM((27, 32, 512), F32), pltpu.SemaphoreType.DMA((29,))],
        compiler_params=pltpu.CompilerParams(vmem_limit_bytes=40 * 1024 * 1024),
    )(resp, vgrad, kcode)
    return (resp.reshape(volume.shape), vgrad.reshape(volume.shape), kgrad)


def solution(mesh):
    in_specs = (P("ch", None, "sx", "sy"), P(None, "ch", None), P("ch", None, "sx", "sy"))
    out_specs = (P("ch", None, "sx", "sy"), P("ch", None, "sx", "sy"), P(None, "ch", None))
    return jax.shard_map(shards, mesh=mesh, in_specs=in_specs, out_specs=out_specs, check_vma=False)
```
